32 devices in a mesh: dp: 16 (over z, x, core), tensor: 2 (over y).
Axes of the slice: x: 2, y: 2, z: 4, core: 2. Of those that a mesh axis runs over, the one named last changes fastest.
Arguments:
- tokens: bfloat16 [6304, 768], P(('dp', 'tensor')), may hold values from -6 to 6
- w_qkv: bfloat16 [768, 3, 768], P('dp', None, 'tensor'), may hold values from -0.21875 to 0.21875
- w_mix: bfloat16 [768, 768], P('dp', 'tensor'), may hold values from -0.875 to 0.875
- w_router: bfloat16 [768, 16], P('dp'), may hold values from -0.15625 to 0.15625
- gain_one: bfloat16 [768], P('dp'), may hold values from 0.5 to 1.5
- shift_one: bfloat16 [768], P('dp'), may hold values from -1 to 1
- gain_two: bfloat16 [768], P('dp'), may hold values from 0.5 to 1.5
- shift_two: bfloat16 [768], P('dp'), may hold values from -1 to 1
- w_expand: bfloat16 [16, 768, 3072], P('dp', None, 'tensor'), may hold values from -0.21875 to 0.21875
- w_shrink: bfloat16 [16, 3072, 768], P('dp', 'tensor'), may hold values from -0.109375 to 0.109375
- expert_ids: int32 [6304, 2], P('dp'), may hold values from 0 to 15, as said below
- slot_ids: int32 [6304, 2], P('dp'), may hold values from 0 to 63, as said below
- keep_mask: int32 [6304, 2], P('dp'), may hold values from 0 to 1
- out_grad: bfloat16 [6304, 768], P(('dp', 'tensor')), may hold values from -6 to 6
Outputs:
- block_out: bfloat16 [6304, 768], P(('dp', 'tensor'))
- grad_tokens: float32 [6304, 768], P(('dp', 'tensor'))
- grad_w_qkv: float32 [768, 3, 768], P('dp', None, 'tensor')
- grad_w_mix: float32 [768, 768], P('dp', 'tensor')
- grad_router: float32 [768, 16], P(('dp', 'tensor'))
- grad_gain_one: float32 [768], P(('dp', 'tensor'))
- grad_shift_one: float32 [768], P(('dp', 'tensor'))
- grad_gain_two: float32 [768], P(('dp', 'tensor'))
- grad_shift_two: float32 [768], P(('dp', 'tensor'))
- grad_w_expand: float32 [16, 768, 3072], P('dp', None, 'tensor')
- grad_w_shrink: float32 [16, 3072, 768], P('dp', 'tensor')
The draws below stay inside these ranges and needn't reach their ends.
Inputs may be any that keep to these rules, and one draw needn't show every extreme that they name: `expert_ids`: the two experts of a token differ. `slot_ids`: among the kept routes of the 394 rows of one index of dp, no two share an expert and a slot; a dropped route has slot 0.
All inputs are finite; a program needn't handle non-finite values.
Results may differ from the reference program's by a relative error of at most 0.017.
Values may be sent and summed in bfloat16 or wider, within the bound.
A program may use at most 128 MiB of HBM per device.

```python
import jax
import jax.numpy as jnp
from jax import lax

D = 768
H = 12
DH = 64
FF = 3072
SEQ = 197
IMG_DEV = 2
TOK_GROUP = 394
TOKENS = 6304
EXPERTS = 16
SLOT = 64
N_DP = 16
N_TENSOR = 2


def route_plan(key):
    key = jax.random.fold_in(key, 11)
    first_key, second_key, hot_key, order_key = jax.random.split(key, 4)
    first = jax.random.randint(first_key, (N_DP, TOK_GROUP), 0, EXPERTS)
    offset = jax.random.randint(second_key, (N_DP, TOK_GROUP), 1, EXPERTS)
    hottest = jax.random.randint(hot_key, (), 0, EXPERTS)
    order = jax.vmap(lambda sub_key: jax.random.permutation(sub_key, TOK_GROUP))(jax.random.split(order_key, N_DP))
    crowd = SLOT + SLOT // 4 + 1
    first = jnp.where(order < crowd, hottest, first)
    second = (first + offset) % EXPERTS
    chosen = jnp.stack([first, second], -1).reshape(N_DP, 2 * TOK_GROUP)
    onehot = (chosen[:, :, None] == jnp.arange(EXPERTS)[None, None, :]).astype(jnp.int32)
    before = jnp.cumsum(onehot, axis=1) - onehot
    rank = jnp.sum(before * onehot, axis=2)
    keep = (rank < SLOT).astype(jnp.int32)
    slot = jnp.where(keep > 0, rank, 0)
    return (chosen.reshape(TOKENS, 2).astype(jnp.int32), slot.reshape(TOKENS, 2).astype(jnp.int32), keep.reshape(TOKENS, 2))


def draw_expert_ids(key, part):
    return route_plan(key)[0]


def draw_slot_ids(key, part):
    return route_plan(key)[1]


def draw_keep_mask(key, part):
    return route_plan(key)[2]


def with_spikes(values, rng, source, target, shards_of, factor):
    owner, partner = [(jnp.arange(values.shape[axis_at]) // (values.shape[axis_at] // shards_of)).reshape([-1 if axis == axis_at else 1 for axis in range(values.ndim)]) for axis_at in (source, target)]
    chosen = jax.random.permutation(rng, shards_of)[partner]
    strong = (owner == chosen) | (owner == (partner + shards_of // 2) % shards_of)
    return jnp.where(strong, factor * values, values)


def level_of(key, shape, cuts, low, largest):
    level, own = 1.0, jax.random.fold_in(key, 6)
    for position, shards_of in cuts:
        steps = jnp.exp(jax.random.uniform(jax.random.fold_in(own, position), (shards_of,), jnp.float32, low / len(cuts), largest / len(cuts)))
        level = level * jnp.repeat(steps, shape[position] // shards_of).reshape([-1 if axis == position else 1 for axis in range(len(shape))])
    return level


def noise(stream_key, extent, deviation, most, pieces=(), held_as=jnp.bfloat16):
    level = level_of(stream_key, extent, pieces, -0.22, 0.18) if pieces else 1.0
    array = jax.random.normal(stream_key, extent, jnp.float32) * deviation * level
    return jnp.minimum(jnp.maximum(array, -most), most).astype(held_as)


def gaussian_with(key, dims, width, most, cuts, heavy, kind=jnp.bfloat16):
    drawn = width * jax.random.normal(key, dims, jnp.float32)
    if cuts:
        drawn = drawn * level_of(key, dims, cuts, -0.22, 0.18)
    return jnp.clip(with_spikes(drawn, jax.random.fold_in(key, 3), *heavy), -most, most).astype(kind)


def setup_inputs(seed: int = 0) -> dict:
    key_of = jax.random.split(jax.random.key(seed), 15)
    return {
        "tokens": noise(key_of[0], (TOKENS, D), 1.0, 6.0, ((0, 32),)),
        "w_qkv": noise(key_of[1], (D, 3, D), D ** -0.5, 0.21875, ((0, 16), (2, 2))),
        "w_mix": noise(key_of[2], (D, D), (D // 16) ** -0.5, 0.875, ((0, 16), (1, 2))),
        "w_router": noise(key_of[3], (D, EXPERTS), (2 * D) ** -0.5, 0.15625, ((0, 16),)),
        "gain_one": jnp.clip(1.0 + 0.1 * jax.random.normal(key_of[4], (D,), jnp.float32), 0.5, 1.5).astype(jnp.bfloat16),
        "shift_one": noise(key_of[5], (D,), 0.2, 1.0, ((0, 16),)),
        "gain_two": jnp.clip(1.0 + 0.1 * jax.random.normal(key_of[6], (D,), jnp.float32), 0.5, 1.5).astype(jnp.bfloat16),
        "shift_two": noise(key_of[7], (D,), 0.2, 1.0, ((0, 16),)),
        "w_expand": noise(key_of[8], (EXPERTS, D, FF), D ** -0.5, 0.21875, ((0, 16), (2, 2))),
        "w_shrink": noise(key_of[9], (EXPERTS, FF, D), FF ** -0.5, 0.109375, ((0, 16), (1, 2))),
        "expert_ids": draw_expert_ids(jax.random.fold_in(key_of[14], 71), 0),
        "slot_ids": draw_slot_ids(jax.random.fold_in(key_of[14], 71), 0),
        "keep_mask": draw_keep_mask(jax.random.fold_in(key_of[14], 71), 0),
        "out_grad": gaussian_with(key_of[13], (TOKENS, D), 1.0, 6.0, ((0, 32),), (0, 1, 32, 2.75)),
    }


@jax.custom_vjp
def low(v):
    return lax.optimization_barrier(v.astype(jnp.bfloat16)).astype(jnp.float32)

@jax.custom_vjp
def low_back(v):
    return v

def low_keep(v):
    return (low(v), None)

def low_pass(kept, grad):
    return (grad,)

def back_keep(v):
    return (v, None)

def back_low(kept, grad):
    return (low(grad),)
low.defvjp(low_keep, low_pass)
low_back.defvjp(back_keep, back_low)

def norm_rows(values, gain, shift):
    centre = values - lax.optimization_barrier(jnp.mean(values, axis=-1, keepdims=True))
    spread = lax.optimization_barrier(jnp.mean(centre * centre, axis=-1, keepdims=True))
    return centre * lax.rsqrt(spread + 1e-06) * gain + shift

def reference(tokens, w_qkv, w_mix, w_router, gain_one, shift_one, gain_two, shift_two, w_expand, w_shrink, expert_ids, slot_ids, keep_mask, out_grad):
    highest = lax.Precision.HIGHEST
    capacity = SLOT * N_DP
    keep_float = keep_mask.astype(jnp.float32)
    route_index = jnp.arange(TOKENS * 2, dtype=jnp.int32).reshape(TOKENS, 2)
    group_index = (jnp.arange(TOKENS, dtype=jnp.int32) // TOK_GROUP)[:, None]
    dest = jnp.where(keep_mask > 0, expert_ids * capacity + group_index * SLOT + slot_ids, EXPERTS * capacity).astype(jnp.int32)
    table = jnp.full((EXPERTS * capacity + 1,), 2 * TOKENS, jnp.int32)
    table = table.at[dest.reshape(-1)].set(route_index.reshape(-1))[:-1].reshape(EXPERTS, capacity)
    half = FF // N_TENSOR
    scale = DH ** (-0.5)

    def forward(resid, qkv_w, mix_w, router_w, gain_a, shift_a, gain_b, shift_b, expand_w, shrink_w):
        normed_a = low(norm_rows(resid, gain_a, shift_a))

        def attention_block(rows):
            raw = jnp.einsum('rd,dcf->rcf', rows, qkv_w, precision=highest)
            mixed = low(low_back(raw))
            shaped = mixed.reshape(IMG_DEV, SEQ, 3, H, DH)
            query = shaped[:, :, 0]
            key_rows = shaped[:, :, 1]
            value_rows = shaped[:, :, 2]
            scores = low_back(jnp.einsum('ishd,ithd->ihst', query, key_rows, precision=highest) * scale)
            probs = low(jax.nn.softmax(scores, axis=-1))
            heads = jnp.einsum('ihst,ithd->ishd', probs, value_rows, precision=highest).reshape(TOK_GROUP, H * DH)
            heads = low(low_back(heads))
            return jnp.einsum('rf,of->ro', heads, mix_w, precision=highest)
        branch_a = lax.map(jax.checkpoint(attention_block), normed_a.reshape(N_DP, TOK_GROUP, D)).reshape(TOKENS, D)
        branch_a = low_back(branch_a)
        resid_b = resid + branch_a
        normed_b = low(norm_rows(resid_b, gain_b, shift_b))
        logits = jnp.dot(normed_b, router_w, precision=highest)
        chosen = jnp.take_along_axis(logits, expert_ids, axis=1)
        gates = jax.nn.softmax(chosen, axis=-1) * keep_float
        padded = jnp.concatenate([normed_b, jnp.zeros((1, D), jnp.float32)], 0)

        def expert_block(items):
            index, expand, shrink = items
            rows = jnp.take(padded, index // 2, axis=0)
            total = jnp.zeros((capacity, D), jnp.float32)
            for part in range(N_TENSOR):
                inputs = low_back(rows)
                inner = low_back(jnp.dot(inputs, expand[:, part * half:(part + 1) * half], precision=highest))
                active = low(jax.nn.gelu(inner))
                total = total + low(low_back(jnp.dot(active, shrink[part * half:(part + 1) * half], precision=highest)))
            return total
        outputs = lax.map(jax.checkpoint(expert_block), (table, expand_w, shrink_w))
        flat = jnp.concatenate([outputs.reshape(-1, D), jnp.zeros((1, D), jnp.float32)], 0)
        route_out = jnp.take(flat, dest.reshape(-1), axis=0).reshape(TOKENS, 2, D)
        branch_b = lax.optimization_barrier(jnp.sum(gates[:, :, None] * route_out, axis=1))
        return resid_b + branch_b
    primals = (tokens.astype(jnp.float32), w_qkv.astype(jnp.float32), w_mix.astype(jnp.float32), w_router.astype(jnp.float32), gain_one.astype(jnp.float32), shift_one.astype(jnp.float32), gain_two.astype(jnp.float32), shift_two.astype(jnp.float32), w_expand.astype(jnp.float32), w_shrink.astype(jnp.float32))
    final, pull = jax.vjp(forward, *primals)
    grads = pull(out_grad.astype(jnp.float32))
    return (final.astype(jnp.bfloat16), grads[0], grads[1], grads[2], grads[3], grads[4], grads[5], grads[6], grads[7], grads[8], grads[9])
```

```python
import functools

import jax
import jax.numpy as jnp
from jax import lax
from jax.experimental import pallas as pl
from jax.experimental.pallas import tpu as pltpu
from jax.sharding import PartitionSpec as P

DH = 64
SEQ = 197
MESH = pl.DeviceIdType.MESH
VMEM = pl.BlockSpec(memory_space=pltpu.VMEM)
LIMIT = 48 * 1024 * 1024


def greet(peers):
    barrier = pltpu.get_barrier_semaphore()
    for peer in peers:
        pl.semaphore_signal(barrier, inc=1, device_id=peer, device_id_type=MESH)
    pl.semaphore_wait(barrier, len(peers))


def remote(src, dst, send, recv, peer):
    return pltpu.make_async_remote_copy(
        src_ref=src,
        dst_ref=dst,
        send_sem=send,
        recv_sem=recv,
        device_id=peer,
        device_id_type=MESH,
    )


def flip(me, mask):
    place = me
    bit = 1
    while bit <= mask:
        if mask & bit:
            place = place + bit - 2 * bit * lax.rem(me // bit, 2)
        bit *= 2
    return place


def low_bit(mask, n):
    return (mask & -mask) if mask else n


def bits_below(limit):
    bits = []
    bit = 1
    while bit < limit:
        bits.append(bit)
        bit *= 2
    return bits


def call(kernel, ident, outs, scratch, *operands):
    return pl.pallas_call(
        kernel,
        out_shape=outs,
        in_specs=[VMEM] * len(operands),
        out_specs=[VMEM] * len(outs),
        scratch_shapes=scratch,
        compiler_params=pltpu.CompilerParams(
            collective_id=ident, has_side_effects=True, vmem_limit_bytes=LIMIT
        ),
    )(*operands)


def shape_of(array):
    return jax.ShapeDtypeStruct(array.shape, array.dtype)


def swap_kernel(count, *refs):
    ins, outs = refs[:count], refs[count : 2 * count]
    send, recv = refs[2 * count :]
    other = {"tensor": 1 - lax.axis_index("tensor")}
    greet([other])
    copies = [remote(ins[i], outs[i], send.at[i], recv.at[i], other) for i in range(count)]
    for copy in copies:
        copy.start()
    for copy in copies:
        copy.wait()


def swap(ident, *arrays):
    count = len(arrays)
    return call(
        functools.partial(swap_kernel, count),
        ident,
        [shape_of(array) for array in arrays],
        [pltpu.SemaphoreType.DMA((count,)), pltpu.SemaphoreType.DMA((count,))],
        *arrays,
    )


def gather_kernel(n, shard, rows_a, rows_b, full, other_a, other_b, send, recv, pair_send, pair_recv, own):
    me = lax.axis_index("dp")
    other = {"tensor": 1 - lax.axis_index("tensor")}
    bits = bits_below(n)
    greet([{"dp": flip(me, bit)} for bit in bits] + [other])
    pair = [
        remote(rows_a, other_a, pair_send.at[0], pair_recv.at[0], other),
        remote(rows_b, other_b, pair_send.at[1], pair_recv.at[1], other),
    ]

    def hop(mask, bit):
        owner = flip(me, mask)
        src = shard if mask == 0 else full.at[owner]
        index = mask | bit
        return remote(
            src, full.at[owner], send.at[index], recv.at[index], {"dp": flip(me, bit)}
        )

    keep = pltpu.make_async_copy(shard, full.at[me], own)
    order = sorted(range(n), key=lambda mask: (-low_bit(mask, n), mask))
    sent = []
    for mask in order:
        if mask:
            bit = low_bit(mask, n)
            hop(mask ^ bit, bit).wait_recv()
        for bit in reversed(bits_below(low_bit(mask, n))):
            copy = hop(mask, bit)
            copy.start()
            sent.append(copy)
        if mask == 0:
            for copy in pair:
                copy.start()
            keep.start()
    keep.wait()
    for copy in sent:
        copy.wait_send()
    for copy in pair:
        copy.wait()


def gather(n, shard, rows_a, rows_b):
    return call(
        functools.partial(gather_kernel, n),
        1,
        [
            jax.ShapeDtypeStruct((n,) + shard.shape, shard.dtype),
            shape_of(rows_a),
            shape_of(rows_b),
        ],
        [
            pltpu.SemaphoreType.DMA((n,)),
            pltpu.SemaphoreType.DMA((n,)),
            pltpu.SemaphoreType.DMA((2,)),
            pltpu.SemaphoreType.DMA((2,)),
            pltpu.SemaphoreType.DMA,
        ],
        shard,
        rows_a,
        rows_b,
    )


def everyone(n, me):
    return [{"dp": lax.rem(me + k, n)} for k in range(1, n)] + [
        {"tensor": 1 - lax.axis_index("tensor")}
    ]


def dispatch_kernel(n, in_a, in_b, out_a, out_b, send, recv, pair_send, pair_recv, own):
    me = lax.axis_index("dp")
    half = lax.axis_index("tensor")
    other = {"tensor": 1 - half}
    width = in_a.shape[2]
    columns = pl.ds(pl.multiple_of(half * width, 128), width)
    ins, outs = (in_a, in_b), (out_a, out_b)
    greet(everyone(n, me))

    def direct(i, k):
        peer = lax.rem(me + k, n)
        return remote(
            ins[i].at[peer],
            outs[i].at[me, :, columns],
            send.at[i, k],
            recv.at[i, k],
            {"dp": peer},
        )

    def onward(i, k):
        part = outs[i].at[lax.rem(me - k + n, n), :, columns]
        return remote(part, part, pair_send.at[i, k], pair_recv.at[i, k], other)

    keep = [
        pltpu.make_async_copy(ins[i].at[me], outs[i].at[me, :, columns], own.at[i])
        for i in range(2)
    ]
    for i in range(2):
        keep[i].start()
        for k in range(1, n):
            direct(i, k).start()
    for i in range(2):
        keep[i].wait()
        onward(i, 0).start()
        for k in range(1, n):
            direct(i, k).wait_recv()
            onward(i, k).start()
    for i in range(2):
        for k in range(1, n):
            direct(i, k).wait_send()
        for k in range(n):
            onward(i, k).wait()


def dispatch(n, rows_a, rows_b):
    full = jax.ShapeDtypeStruct(rows_a.shape[:2] + (2 * rows_a.shape[2],), rows_a.dtype)
    return call(
        functools.partial(dispatch_kernel, n),
        2,
        [full, full],
        [pltpu.SemaphoreType.DMA((2, n)) for _ in range(4)] + [pltpu.SemaphoreType.DMA((2,))],
        rows_a,
        rows_b,
    )


def combine_kernel(
    n, in_a, in_b, out_a, out_b, got_a, got_b, sum_a, sum_b, send, recv, pair_send, pair_recv, own
):
    me = lax.axis_index("dp")
    half = lax.axis_index("tensor")
    other = {"tensor": 1 - half}
    width = out_a.shape[2]
    theirs = pl.ds(pl.multiple_of((1 - half) * width, 128), width)
    mine = pl.ds(pl.multiple_of(half * width, 128), width)
    ins, outs, gots, sums = (in_a, in_b), (out_a, out_b), (got_a, got_b), (sum_a, sum_b)
    greet(everyone(n, me))

    def across(i, k):
        block = lax.rem(me + k, n)
        return remote(
            ins[i].at[block, :, theirs],
            gots[i].at[block],
            pair_send.at[i, k],
            pair_recv.at[i, k],
            other,
        )

    def home(i, k):
        block = lax.rem(me + k, n)
        return remote(
            sums[i].at[block], outs[i].at[me], send.at[i, k], recv.at[i, k], {"dp": block}
        )

    order = list(range(1, n)) + [0]
    for i in range(2):
        for k in order:
            across(i, k).start()
    for i in range(2):
        for k in order:
            across(i, k).wait_recv()
            block = lax.rem(me + k, n)
            kept = ins[i][block, :, mine].astype(jnp.float32)
            total = (kept + gots[i][block].astype(jnp.float32)).astype(jnp.bfloat16)
            if k:
                sums[i][block] = total
                home(i, k).start()
            else:
                outs[i][block] = total
    for i in range(2):
        for k in range(n):
            across(i, k).wait_send()
        for k in range(1, n):
            home(i, k).wait()


def combine(n, parts_a, parts_b):
    size = parts_a.shape[:2] + (parts_a.shape[2] // 2,)
    out = jax.ShapeDtypeStruct(size, parts_a.dtype)
    return call(
        functools.partial(combine_kernel, n),
        3,
        [out, out],
        [pltpu.VMEM(size, parts_a.dtype) for _ in range(4)]
        + [pltpu.SemaphoreType.DMA((2, n)) for _ in range(4)]
        + [pltpu.SemaphoreType.DMA((2,))],
        parts_a,
        parts_b,
    )


def reduce_kernel(
    n, small, grads, rows, out, out_small, out_rows, got, stage, mine, theirs, send, recv, pair_send, pair_recv
):
    me = lax.axis_index("dp")
    other = {"tensor": 1 - lax.axis_index("tensor")}
    greet([{"dp": flip(me, bit)} for bit in bits_below(n)] + [other])
    pair_rows = remote(rows, out_rows, pair_send.at[0], pair_recv.at[0], other)
    pair_rows.start()

    def hop(mask):
        bit = low_bit(mask, n)
        src = grads.at[flip(me, mask)] if bit == 1 else stage.at[mask]
        return remote(src, got.at[mask], send.at[mask], recv.at[mask], {"dp": flip(me, bit)})

    def total(mask):
        value = grads[flip(me, mask)].astype(jnp.float32)
        for bit in bits_below(low_bit(mask, n)):
            hop(mask | bit).wait_recv()
            value = value + got[mask | bit].astype(jnp.float32)
        return value

    order = sorted(
        range(1, n), key=lambda mask: (low_bit(mask, n), low_bit(mask ^ low_bit(mask, n), n))
    )
    for mask in order:
        if low_bit(mask, n) > 1:
            stage[mask] = total(mask).astype(stage.dtype)
        hop(mask).start()
    value = total(0)
    out[...] = value
    mine[...] = value[:, value.shape[1] - small :]
    pair_small = remote(mine, theirs, pair_send.at[1], pair_recv.at[1], other)
    pair_small.start()
    for mask in order:
        hop(mask).wait_send()
    pair_small.wait()
    out_small[...] = mine[...] + theirs[...]
    pair_rows.wait()


def reduce(n, small, grads, rows):
    depth, columns = grads.shape[1:]
    return call(
        functools.partial(reduce_kernel, n, small),
        4,
        [
            jax.ShapeDtypeStruct((depth, columns), jnp.float32),
            jax.ShapeDtypeStruct((depth, small), jnp.float32),
            shape_of(rows),
        ],
        [
            pltpu.VMEM(grads.shape, grads.dtype),
            pltpu.VMEM(grads.shape, grads.dtype),
            pltpu.VMEM((depth, small), jnp.float32),
            pltpu.VMEM((depth, small), jnp.float32),
            pltpu.SemaphoreType.DMA((n,)),
            pltpu.SemaphoreType.DMA((n,)),
            pltpu.SemaphoreType.DMA((2,)),
            pltpu.SemaphoreType.DMA((2,)),
        ],
        grads,
        rows,
    )


def in_order(half, mine, theirs, axis):
    first = jnp.where(half == 0, mine, theirs)
    second = jnp.where(half == 0, theirs, mine)
    return jnp.concatenate([first, second], axis=axis)


def norm_rows(values, gain, shift):
    centre = values - jnp.mean(values, axis=-1, keepdims=True)
    spread = jnp.mean(centre * centre, axis=-1, keepdims=True)
    return centre * lax.rsqrt(spread + 1e-06) * gain + shift


def split_heads(mixed, images, head_size):
    heads = mixed.shape[2] // head_size
    shaped = mixed.reshape(images, -1, 3, heads, head_size)
    return (shaped[:, :, 0], shaped[:, :, 1], shaped[:, :, 2])


def attend(mixed, images, head_size):
    query, key_rows, value_rows = split_heads(mixed, images, head_size)
    scores = jnp.einsum(
        "ishd,ithd->ihst", query, key_rows, preferred_element_type=jnp.float32
    ) * head_size ** (-0.5)
    highest_score = jnp.max(scores, axis=-1, keepdims=True)
    total = jnp.sum(jnp.exp(scores - highest_score), axis=-1, keepdims=True)
    log_total = highest_score + jnp.log(total)
    weights = jnp.exp(scores - log_total).astype(jnp.bfloat16)
    heads_out = jnp.einsum(
        "ihst,ithd->ishd", weights, value_rows, preferred_element_type=jnp.float32
    )
    return (heads_out.reshape(mixed.shape[0], -1).astype(jnp.bfloat16), log_total)


def attend_back(mixed, log_total, grad_heads, images, head_size):
    query, key_rows, value_rows = split_heads(mixed, images, head_size)
    scale = head_size ** (-0.5)
    scores = (
        jnp.einsum("ishd,ithd->ihst", query, key_rows, preferred_element_type=jnp.float32) * scale
    )
    probs = jnp.exp(scores - log_total)
    weights = probs.astype(jnp.bfloat16)
    grad_shaped = grad_heads.reshape(query.shape)
    grad_weights = jnp.einsum(
        "ishd,ithd->ihst", grad_shaped, value_rows, preferred_element_type=jnp.float32
    )
    grad_values = jnp.einsum(
        "ihst,ishd->ithd", weights, grad_shaped, preferred_element_type=jnp.float32
    )
    grad_scores = (
        probs * (grad_weights - jnp.sum(probs * grad_weights, axis=-1, keepdims=True))
    ).astype(jnp.bfloat16)
    grad_query = (
        jnp.einsum("ihst,ithd->ishd", grad_scores, key_rows, preferred_element_type=jnp.float32)
        * scale
    )
    grad_keys = (
        jnp.einsum("ihst,ishd->ithd", grad_scores, query, preferred_element_type=jnp.float32)
        * scale
    )
    stacked = jnp.stack([grad_query, grad_keys, grad_values], axis=2)
    return stacked.reshape(mixed.shape[0], 3, -1)


def body(
    tokens,
    w_qkv,
    w_mix,
    w_router,
    gain_one,
    shift_one,
    gain_two,
    shift_two,
    w_expand,
    w_shrink,
    expert_ids,
    slot_ids,
    keep_mask,
    out_grad,
):
    highest = lax.Precision.HIGHEST
    contract_rows = (((0,), (0,)), ((), ()))
    contract_cols = (((1,), (1,)), ((), ()))
    bf16 = jnp.bfloat16
    f32 = jnp.float32
    rows, width = tokens.shape
    group = expert_ids.shape[0]
    images = group // SEQ
    experts = lax.axis_size("dp")
    half = lax.axis_index("tensor")
    slots = 2 * max(1, 2 * group * 2 // 3 // experts)
    depth = w_qkv.shape[0]
    qkv_cols = 3 * w_qkv.shape[2]
    mix_cols = w_mix.shape[1]
    half_width = width // 2
    small = -(-(experts + 4) // 128) * 128

    vectors = jnp.stack([gain_one, shift_one, gain_two, shift_two], axis=1)
    shard = jnp.concatenate(
        [
            w_qkv.reshape(depth, qkv_cols),
            w_mix,
            w_router,
            vectors,
            jnp.zeros((depth, small - experts - 4), bf16),
        ],
        axis=1,
    )
    full, tokens_other, grad_other = gather(experts, shard, tokens, out_grad)
    full = full.reshape(experts * depth, -1)
    qkv_full = full[:, :qkv_cols]
    mix_full = full[:, qkv_cols : qkv_cols + mix_cols]
    router_full = full[:, qkv_cols + mix_cols : qkv_cols + mix_cols + experts]
    vectors = full[:, qkv_cols + mix_cols + experts : qkv_cols + mix_cols + experts + 4]
    gain_a, shift_a, gain_b, shift_b = vectors.astype(f32).T
    resid = in_order(half, tokens, tokens_other, 0).astype(f32)
    grad_group = in_order(half, out_grad, grad_other, 0).astype(f32)

    group_a = norm_rows(resid, gain_a, shift_a).astype(bf16)
    mixed = (
        jnp.dot(group_a, qkv_full, preferred_element_type=f32).astype(bf16).reshape(group, 3, -1)
    )
    heads_out, log_total = attend(mixed, images, DH)
    branch = lax.dot_general(
        heads_out, mix_full, contract_cols, preferred_element_type=f32
    ).astype(bf16)
    (branch_other,) = swap(5, branch)
    resid_b = resid + (branch.astype(f32) + branch_other.astype(f32))
    group_b = norm_rows(resid_b, gain_b, shift_b).astype(bf16)

    logits = jnp.dot(group_b, router_full, preferred_element_type=f32)
    onehot = expert_ids[:, :, None] == jnp.arange(experts, dtype=jnp.int32)[None, None, :]
    chosen = jnp.sum(jnp.where(onehot, logits[:, None, :], 0.0), axis=-1)
    pick = jax.nn.softmax(chosen, axis=-1)
    keep_float = keep_mask.astype(f32)
    gates = pick * keep_float
    dest = jnp.where(keep_mask > 0, expert_ids * slots + slot_ids, experts * slots)
    places = jnp.arange(experts * slots, dtype=jnp.int32)[None, :]
    spread = [(dest[:, j : j + 1] == places).astype(bf16) for j in range(2)]
    spread_both = spread[0] + spread[1]

    def my_columns(values):
        return lax.dynamic_slice_in_dim(values, half * half_width, half_width, 1)

    rows_sent = lax.dot_general(
        spread_both, my_columns(group_b), contract_rows, preferred_element_type=f32
    ).astype(bf16)
    grad_cols = my_columns(grad_group)
    grads_sent = sum(
        lax.dot_general(
            spread[j],
            (gates[:, j : j + 1] * grad_cols).astype(bf16),
            contract_rows,
            preferred_element_type=f32,
        )
        for j in range(2)
    ).astype(bf16)
    arrived, grad_result = dispatch(
        experts,
        rows_sent.reshape(experts, slots, half_width),
        grads_sent.reshape(experts, slots, half_width),
    )
    arrived = arrived.reshape(-1, width)
    grad_result = grad_result.reshape(-1, width)

    expand_here = w_expand[0]
    shrink_here = w_shrink[0]
    inner = jnp.dot(arrived, expand_here, preferred_element_type=f32)
    gelu_value, gelu_pull = jax.vjp(jax.nn.gelu, inner)
    active = gelu_value.astype(bf16)
    result = jnp.dot(active, shrink_here, preferred_element_type=f32).astype(bf16)
    grad_active = lax.dot_general(
        grad_result, shrink_here, contract_cols, preferred_element_type=f32
    )
    grad_inner = gelu_pull(grad_active)[0].astype(bf16)
    grad_arrived = lax.dot_general(
        grad_inner, expand_here, contract_cols, preferred_element_type=f32
    ).astype(bf16)
    back, grad_back = combine(
        experts,
        result.reshape(experts, slots, width),
        grad_arrived.reshape(experts, slots, width),
    )
    grad_shrink = lax.dot_general(active, grad_result, contract_rows, preferred_element_type=f32)
    grad_expand = lax.dot_general(arrived, grad_inner, contract_rows, preferred_element_type=f32)

    back = back.reshape(-1, half_width)
    grad_back = grad_back.reshape(-1, half_width)
    route_out = [jnp.dot(spread[j], back, preferred_element_type=f32) for j in range(2)]
    branch_cols = (gates[:, 0:1] * route_out[0] + gates[:, 1:2] * route_out[1]).astype(bf16)
    gate_part = jnp.stack([jnp.sum(grad_cols * route_out[j], axis=-1) for j in range(2)], axis=0)
    grad_cols_b = jnp.dot(spread_both, grad_back, preferred_element_type=f32).astype(bf16)
    branch_theirs, grad_theirs, gate_theirs = swap(6, branch_cols, grad_cols_b, gate_part)
    grad_gate = (gate_part + gate_theirs).T
    branch_b = in_order(half, branch_cols, branch_theirs, 1).astype(f32)
    grad_routes = in_order(half, grad_cols_b, grad_theirs, 1).astype(f32)
    block_out = lax.dynamic_slice_in_dim(resid_b + branch_b, half * rows, rows, 0).astype(bf16)

    grad_pick = keep_float * grad_gate
    grad_chosen = pick * (grad_pick - jnp.sum(pick * grad_pick, axis=-1, keepdims=True))
    grad_logits = jnp.sum(jnp.where(onehot, grad_chosen[:, :, None], 0.0), axis=1)
    grad_router = lax.dot_general(
        group_b.astype(f32), grad_logits, contract_rows, precision=highest
    )
    grad_normed_b = grad_routes + lax.dot_general(
        grad_logits, router_full.astype(f32), contract_cols, precision=highest
    )
    norm_value_b, norm_pull_b = jax.vjp(norm_rows, resid_b, gain_b, shift_b)
    grad_resid_b, grad_gain_b, grad_shift_b = norm_pull_b(grad_normed_b)
    grad_resid_b = grad_resid_b + grad_group

    grad_branch = grad_resid_b.astype(bf16)
    grad_mix = lax.dot_general(
        grad_branch, heads_out, contract_rows, preferred_element_type=f32
    )
    grad_heads = jnp.dot(grad_branch, mix_full, preferred_element_type=f32).astype(bf16)
    grad_mixed = attend_back(mixed, log_total, grad_heads, images, DH).astype(bf16)
    grad_mixed = grad_mixed.reshape(group, qkv_cols)
    grad_qkv = lax.dot_general(group_a, grad_mixed, contract_rows, preferred_element_type=f32)
    grad_part = lax.dot_general(grad_mixed, qkv_full, contract_cols, preferred_element_type=f32)
    norm_value_a, norm_pull_a = jax.vjp(norm_rows, resid, gain_a, shift_a)
    grad_gain_a, grad_shift_a = norm_pull_a(grad_part)[1:]
    grads = jnp.concatenate(
        [
            grad_qkv.astype(bf16),
            grad_mix.astype(bf16),
            (0.5 * grad_router).astype(bf16),
            jnp.stack(
                [grad_gain_a, grad_shift_a, 0.5 * grad_gain_b, 0.5 * grad_shift_b], axis=1
            ).astype(bf16),
            jnp.zeros((width, small - experts - 4), bf16),
        ],
        axis=1,
    ).reshape(experts, depth, -1)
    part_theirs = lax.dynamic_slice_in_dim(grad_part, (1 - half) * rows, rows, 0).astype(bf16)
    summed, summed_small, part_got = reduce(experts, small, grads, part_theirs)
    summed_small = lax.dynamic_slice_in_dim(summed_small, half * (depth // 2), depth // 2, 0)
    grad_normed_a = lax.dynamic_slice_in_dim(grad_part, half * rows, rows, 0) + part_got.astype(f32)
    own = tokens.astype(f32)
    own_value, own_pull = jax.vjp(lambda values: norm_rows(values, gain_a, shift_a), own)
    grad_tokens = own_pull(grad_normed_a)[0] + lax.dynamic_slice_in_dim(
        grad_resid_b, half * rows, rows, 0
    )
    return (
        block_out,
        grad_tokens,
        summed[:, :qkv_cols].reshape(depth, 3, -1),
        summed[:, qkv_cols : qkv_cols + mix_cols],
        summed_small[:, :experts],
        summed_small[:, experts],
        summed_small[:, experts + 1],
        summed_small[:, experts + 2],
        summed_small[:, experts + 3],
        grad_expand[None],
        grad_shrink[None],
    )


def solution(mesh):
    placed = (
        P(("dp", "tensor"), None),
        P("dp", None, "tensor"),
        P("dp", "tensor"),
        P("dp", None),
        P("dp"),
        P("dp"),
        P("dp"),
        P("dp"),
        P("dp", None, "tensor"),
        P("dp", "tensor", None),
        P("dp", None),
        P("dp", None),
        P("dp", None),
        P(("dp", "tensor"), None),
    )
    return jax.shard_map(
        body,
        mesh=mesh,
        in_specs=placed,
        out_specs=(
            P(("dp", "tensor"), None),
            P(("dp", "tensor"), None),
            P("dp", None, "tensor"),
            P("dp", "tensor"),
            P(("dp", "tensor"), None),
            P(("dp", "tensor")),
            P(("dp", "tensor")),
            P(("dp", "tensor")),
            P(("dp", "tensor")),
            P("dp", None, "tensor"),
            P("dp", "tensor", None),
        ),
        check_vma=False,
    )
```

```python
import functools

import jax
import jax.numpy as jnp
from jax import lax
from jax.experimental import pallas as pl
from jax.experimental.pallas import tpu as pltpu
from jax.sharding import PartitionSpec as P

DH = 64
MESH = pl.DeviceIdType.MESH
VMEM = pl.BlockSpec(memory_space=pltpu.VMEM)
LIMIT = 48 * 1024 * 1024


def greet(peers):
    barrier = pltpu.get_barrier_semaphore()
    for peer in peers:
        pl.semaphore_signal(barrier, inc=1, device_id=peer, device_id_type=MESH)
    pl.semaphore_wait(barrier, len(peers))


def remote(src, dst, send, recv, peer):
    return pltpu.make_async_remote_copy(
        src_ref=src,
        dst_ref=dst,
        send_sem=send,
        recv_sem=recv,
        device_id=peer,
        device_id_type=MESH,
    )


def flip(me, mask):
    place = me
    bit = 1
    while bit <= mask:
        if mask & bit:
            place = place + bit - 2 * bit * lax.rem(me // bit, 2)
        bit *= 2
    return place


def low_bit(mask, n):
    return (mask & -mask) if mask else n


def bits_below(limit):
    bits = []
    bit = 1
    while bit < limit:
        bits.append(bit)
        bit *= 2
    return bits


def call(kernel, ident, outs, scratch, *operands):
    return pl.pallas_call(
        kernel,
        out_shape=outs,
        in_specs=[VMEM] * len(operands),
        out_specs=[VMEM] * len(outs),
        scratch_shapes=scratch,
        compiler_params=pltpu.CompilerParams(
            collective_id=ident, has_side_effects=True, vmem_limit_bytes=LIMIT
        ),
    )(*operands)


def shape_of(array):
    return jax.ShapeDtypeStruct(array.shape, array.dtype)


def swap_kernel(count, *refs):
    ins, outs = refs[:count], refs[count : 2 * count]
    send, recv = refs[2 * count :]
    other = {"tensor": 1 - lax.axis_index("tensor")}
    greet([other])
    copies = [remote(ins[i], outs[i], send.at[i], recv.at[i], other) for i in range(count)]
    for copy in copies:
        copy.start()
    for copy in copies:
        copy.wait()


def swap(ident, *arrays):
    count = len(arrays)
    return call(
        functools.partial(swap_kernel, count),
        ident,
        [shape_of(array) for array in arrays],
        [pltpu.SemaphoreType.DMA((count,)), pltpu.SemaphoreType.DMA((count,))],
        *arrays,
    )


def gather_kernel(n, shard, rows_a, rows_b, full, other_a, other_b, send, recv, pair_send, pair_recv, own):
    me = lax.axis_index("dp")
    other = {"tensor": 1 - lax.axis_index("tensor")}
    bits = bits_below(n)
    greet([{"dp": flip(me, bit)} for bit in bits] + [other])
    pair = [
        remote(rows_a, other_a, pair_send.at[0], pair_recv.at[0], other),
        remote(rows_b, other_b, pair_send.at[1], pair_recv.at[1], other),
    ]

    def hop(mask, bit):
        owner = flip(me, mask)
        src = shard if mask == 0 else full.at[owner]
        index = mask | bit
        return remote(
            src, full.at[owner], send.at[index], recv.at[index], {"dp": flip(me, bit)}
        )

    keep = pltpu.make_async_copy(shard, full.at[me], own)
    order = sorted(range(n), key=lambda mask: (-low_bit(mask, n), mask))
    sent = []
    for mask in order:
        if mask:
            bit = low_bit(mask, n)
            hop(mask ^ bit, bit).wait_recv()
        for bit in reversed(bits_below(low_bit(mask, n))):
            copy = hop(mask, bit)
            copy.start()
            sent.append(copy)
        if mask == 0:
            for copy in pair:
                copy.start()
            keep.start()
    keep.wait()
    for copy in sent:
        copy.wait_send()
    for copy in pair:
        copy.wait()


def gather(n, shard, rows_a, rows_b):
    return call(
        functools.partial(gather_kernel, n),
        1,
        [
            jax.ShapeDtypeStruct((n,) + shard.shape, shard.dtype),
            shape_of(rows_a),
            shape_of(rows_b),
        ],
        [
            pltpu.SemaphoreType.DMA((n,)),
            pltpu.SemaphoreType.DMA((n,)),
            pltpu.SemaphoreType.DMA((2,)),
            pltpu.SemaphoreType.DMA((2,)),
            pltpu.SemaphoreType.DMA,
        ],
        shard,
        rows_a,
        rows_b,
    )


def everyone(n, me):
    return [{"dp": lax.rem(me + k, n)} for k in range(1, n)] + [
        {"tensor": 1 - lax.axis_index("tensor")}
    ]


def dispatch_kernel(n, in_a, in_b, out_a, out_b, send, recv, pair_send, pair_recv, own):
    me = lax.axis_index("dp")
    half = lax.axis_index("tensor")
    other = {"tensor": 1 - half}
    width = in_a.shape[2]
    columns = pl.ds(pl.multiple_of(half * width, 128), width)
    ins, outs = (in_a, in_b), (out_a, out_b)
    greet(everyone(n, me))

    def direct(i, k):
        peer = lax.rem(me + k, n)
        return remote(
            ins[i].at[peer],
            outs[i].at[me, :, columns],
            send.at[i, k],
            recv.at[i, k],
            {"dp": peer},
        )

    def onward(i, k):
        part = outs[i].at[lax.rem(me - k + n, n), :, columns]
        return remote(part, part, pair_send.at[i, k], pair_recv.at[i, k], other)

    keep = [
        pltpu.make_async_copy(ins[i].at[me], outs[i].at[me, :, columns], own.at[i])
        for i in range(2)
    ]
    for i in range(2):
        keep[i].start()
        for k in range(1, n):
            direct(i, k).start()
    for i in range(2):
        keep[i].wait()
        onward(i, 0).start()
        for k in range(1, n):
            direct(i, k).wait_recv()
            onward(i, k).start()
    for i in range(2):
        for k in range(1, n):
            direct(i, k).wait_send()
        for k in range(n):
            onward(i, k).wait()


def dispatch(n, rows_a, rows_b):
    full = jax.ShapeDtypeStruct(rows_a.shape[:2] + (2 * rows_a.shape[2],), rows_a.dtype)
    return call(
        functools.partial(dispatch_kernel, n),
        2,
        [full, full],
        [pltpu.SemaphoreType.DMA((2, n)) for _ in range(4)] + [pltpu.SemaphoreType.DMA((2,))],
        rows_a,
        rows_b,
    )


def combine_kernel(
    n, in_a, in_b, out_a, out_b, got_a, got_b, sum_a, sum_b, send, recv, pair_send, pair_recv, own
):
    me = lax.axis_index("dp")
    half = lax.axis_index("tensor")
    other = {"tensor": 1 - half}
    width = out_a.shape[2]
    theirs = pl.ds(pl.multiple_of((1 - half) * width, 128), width)
    mine = pl.ds(pl.multiple_of(half * width, 128), width)
    ins, outs, gots, sums = (in_a, in_b), (out_a, out_b), (got_a, got_b), (sum_a, sum_b)
    greet(everyone(n, me))

    def across(i, k):
        block = lax.rem(me + k, n)
        return remote(
            ins[i].at[block, :, theirs],
            gots[i].at[block],
            pair_send.at[i, k],
            pair_recv.at[i, k],
            other,
        )

    def home(i, k):
        block = lax.rem(me + k, n)
        return remote(
            sums[i].at[block], outs[i].at[me], send.at[i, k], recv.at[i, k], {"dp": block}
        )

    order = list(range(1, n)) + [0]
    for i in range(2):
        for k in order:
            across(i, k).start()
    for i in range(2):
        for k in order:
            across(i, k).wait_recv()
            block = lax.rem(me + k, n)
            kept = ins[i][block, :, mine].astype(jnp.float32)
            total = (kept + gots[i][block].astype(jnp.float32)).astype(jnp.bfloat16)
            if k:
                sums[i][block] = total
                home(i, k).start()
            else:
                outs[i][block] = total
    for i in range(2):
        for k in range(n):
            across(i, k).wait_send()
        for k in range(1, n):
            home(i, k).wait()


def combine(n, parts_a, parts_b):
    size = parts_a.shape[:2] + (parts_a.shape[2] // 2,)
    out = jax.ShapeDtypeStruct(size, parts_a.dtype)
    return call(
        functools.partial(combine_kernel, n),
        3,
        [out, out],
        [pltpu.VMEM(size, parts_a.dtype) for _ in range(4)]
        + [pltpu.SemaphoreType.DMA((2, n)) for _ in range(4)]
        + [pltpu.SemaphoreType.DMA((2,))],
        parts_a,
        parts_b,
    )


def reduce_kernel(
    n, small, grads, rows, out, out_small, out_rows, got, stage, mine, theirs, send, recv, pair_send, pair_recv
):
    me = lax.axis_index("dp")
    other = {"tensor": 1 - lax.axis_index("tensor")}
    greet([{"dp": flip(me, bit)} for bit in bits_below(n)] + [other])
    pair_rows = remote(rows, out_rows, pair_send.at[0], pair_recv.at[0], other)
    pair_rows.start()

    def hop(mask):
        bit = low_bit(mask, n)
        src = grads.at[flip(me, mask)] if bit == 1 else stage.at[mask]
        return remote(src, got.at[mask], send.at[mask], recv.at[mask], {"dp": flip(me, bit)})

    def total(mask):
        value = grads[flip(me, mask)].astype(jnp.float32)
        for bit in bits_below(low_bit(mask, n)):
            hop(mask | bit).wait_recv()
            value = value + got[mask | bit].astype(jnp.float32)
        return value

    order = sorted(
        range(1, n), key=lambda mask: (low_bit(mask, n), low_bit(mask ^ low_bit(mask, n), n))
    )
    for mask in order:
        if low_bit(mask, n) > 1:
            stage[mask] = total(mask).astype(stage.dtype)
        hop(mask).start()
    value = total(0)
    out[...] = value
    mine[...] = value[:, value.shape[1] - small :]
    pair_small = remote(mine, theirs, pair_send.at[1], pair_recv.at[1], other)
    pair_small.start()
    for mask in order:
        hop(mask).wait_send()
    pair_small.wait()
    out_small[...] = mine[...] + theirs[...]
    pair_rows.wait()


def reduce(n, small, grads, rows):
    depth, columns = grads.shape[1:]
    return call(
        functools.partial(reduce_kernel, n, small),
        4,
        [
            jax.ShapeDtypeStruct((depth, columns), jnp.float32),
            jax.ShapeDtypeStruct((depth, small), jnp.float32),
            shape_of(rows),
        ],
        [
            pltpu.VMEM(grads.shape, grads.dtype),
            pltpu.VMEM(grads.shape, grads.dtype),
            pltpu.VMEM((depth, small), jnp.float32),
            pltpu.VMEM((depth, small), jnp.float32),
            pltpu.SemaphoreType.DMA((n,)),
            pltpu.SemaphoreType.DMA((n,)),
            pltpu.SemaphoreType.DMA((2,)),
            pltpu.SemaphoreType.DMA((2,)),
        ],
        grads,
        rows,
    )


def in_order(half, mine, theirs, axis):
    first = jnp.where(half == 0, mine, theirs)
    second = jnp.where(half == 0, theirs, mine)
    return jnp.concatenate([first, second], axis=axis)


def norm_rows(values, gain, shift):
    centre = values - jnp.mean(values, axis=-1, keepdims=True)
    spread = jnp.mean(centre * centre, axis=-1, keepdims=True)
    return centre * lax.rsqrt(spread + 1e-06) * gain + shift


def softmax_rows(query, key_rows):
    scores = lax.dot_general(
        query, key_rows, (((1,), (1,)), ((), ())), preferred_element_type=jnp.float32
    ) * DH ** (-0.5)
    powers = jnp.exp(scores - jnp.max(scores, axis=-1, keepdims=True))
    return powers / jnp.sum(powers, axis=-1, keepdims=True)


def attend_kernel(wide, normed, full, mixed, heads_out, branch):
    for image in range(normed.shape[0]):
        mixed[image] = jnp.dot(
            normed[image], full[:, : 3 * wide], preferred_element_type=jnp.float32
        ).astype(jnp.bfloat16)
        outs = []
        for at in range(0, wide, DH):
            query, key_rows, value_rows = (
                mixed[image, :, part * wide + at : part * wide + at + DH] for part in range(3)
            )
            weights = softmax_rows(query, key_rows).astype(jnp.bfloat16)
            outs.append(jnp.dot(weights, value_rows, preferred_element_type=jnp.float32))
        heads_out[image] = jnp.concatenate(outs, axis=1).astype(jnp.bfloat16)
        branch[image] = lax.dot_general(
            heads_out[image],
            full[:, 3 * wide : 4 * wide],
            (((1,), (1,)), ((), ())),
            preferred_element_type=jnp.float32,
        ).astype(jnp.bfloat16)


def attend_back_kernel(
    wide, normed, mixed, heads_out, grad_branch, full, grads, grad_part, grad_mixed, grad_heads
):
    rows = (((0,), (0,)), ((), ()))
    cols = (((1,), (1,)), ((), ()))
    f32 = jnp.float32
    scale = DH ** (-0.5)
    for image in range(normed.shape[0]):
        grad_heads[image] = jnp.dot(
            grad_branch[image], full[:, 3 * wide : 4 * wide], preferred_element_type=f32
        ).astype(jnp.bfloat16)
        parts = ([], [], [])
        for at in range(0, wide, DH):
            query, key_rows, value_rows = (
                mixed[image, :, part * wide + at : part * wide + at + DH] for part in range(3)
            )
            probs = softmax_rows(query, key_rows)
            grad_out = grad_heads[image, :, at : at + DH]
            grad_probs = lax.dot_general(grad_out, value_rows, cols, preferred_element_type=f32)
            parts[2].append(
                lax.dot_general(
                    probs.astype(jnp.bfloat16), grad_out, rows, preferred_element_type=f32
                )
            )
            grad_scores = (
                probs * (grad_probs - jnp.sum(probs * grad_probs, axis=-1, keepdims=True))
            ).astype(jnp.bfloat16)
            parts[0].append(jnp.dot(grad_scores, key_rows, preferred_element_type=f32) * scale)
            parts[1].append(
                lax.dot_general(grad_scores, query, rows, preferred_element_type=f32) * scale
            )
        grad_mixed[image] = jnp.concatenate(parts[0] + parts[1] + parts[2], axis=1).astype(
            jnp.bfloat16
        )
        grad_part[image] = lax.dot_general(
            grad_mixed[image], full[:, : 3 * wide], cols, preferred_element_type=f32
        )
    images = range(normed.shape[0])
    grads[:, : 3 * wide] = sum(
        lax.dot_general(normed[i], grad_mixed[i], rows, preferred_element_type=f32) for i in images
    ).astype(jnp.bfloat16)
    grads[:, 3 * wide : 4 * wide] = sum(
        lax.dot_general(grad_branch[i], heads_out[i], rows, preferred_element_type=f32)
        for i in images
    ).astype(jnp.bfloat16)


def local_call(kernel, outs, scratch, *operands):
    return pl.pallas_call(
        kernel,
        out_shape=outs,
        in_specs=[VMEM] * len(operands),
        out_specs=[VMEM] * len(outs),
        scratch_shapes=scratch,
        compiler_params=pltpu.CompilerParams(vmem_limit_bytes=LIMIT),
    )(*operands)


def attend(normed, full, wide):
    images, length, width = normed.shape
    sizes = ((images, length, 3 * wide), (images, length, wide), (images, length, width))
    return local_call(
        functools.partial(attend_kernel, wide),
        [jax.ShapeDtypeStruct(size, jnp.bfloat16) for size in sizes],
        [],
        normed,
        full,
    )


def attend_back(normed, mixed, heads_out, grad_branch, full, wide):
    images, length, width = normed.shape
    return local_call(
        functools.partial(attend_back_kernel, wide),
        [
            jax.ShapeDtypeStruct((width, 4 * wide), jnp.bfloat16),
            jax.ShapeDtypeStruct(normed.shape, jnp.float32),
        ],
        [pltpu.VMEM(mixed.shape, mixed.dtype), pltpu.VMEM(heads_out.shape, heads_out.dtype)],
        normed,
        mixed,
        heads_out,
        grad_branch,
        full,
    )


def body(
    tokens,
    w_qkv,
    w_mix,
    w_router,
    gain_one,
    shift_one,
    gain_two,
    shift_two,
    w_expand,
    w_shrink,
    expert_ids,
    slot_ids,
    keep_mask,
    out_grad,
):
    highest = lax.Precision.HIGHEST
    contract_rows = (((0,), (0,)), ((), ()))
    contract_cols = (((1,), (1,)), ((), ()))
    bf16 = jnp.bfloat16
    f32 = jnp.float32
    rows, width = tokens.shape
    group = expert_ids.shape[0]
    experts = lax.axis_size("dp")
    half = lax.axis_index("tensor")
    slots = 2 * max(1, 2 * group * 2 // 3 // experts)
    depth = w_qkv.shape[0]
    qkv_cols = 3 * w_qkv.shape[2]
    mix_cols = w_mix.shape[1]
    half_width = width // 2
    small = -(-(experts + 4) // 128) * 128

    vectors = jnp.stack([gain_one, shift_one, gain_two, shift_two], axis=1)
    shard = jnp.concatenate(
        [
            w_qkv.reshape(depth, qkv_cols),
            w_mix,
            w_router,
            vectors,
            jnp.zeros((depth, small - experts - 4), bf16),
        ],
        axis=1,
    )
    full, tokens_other, grad_other = gather(experts, shard, tokens, out_grad)
    full = full.reshape(experts * depth, -1)
    router_full = full[:, qkv_cols + mix_cols : qkv_cols + mix_cols + experts]
    vectors = full[:, qkv_cols + mix_cols + experts : qkv_cols + mix_cols + experts + 4]
    gain_a, shift_a, gain_b, shift_b = vectors.astype(f32).T
    resid = in_order(half, tokens, tokens_other, 0).astype(f32)
    grad_group = in_order(half, out_grad, grad_other, 0).astype(f32)

    pictures = jnp.where(
        half == 0, jnp.stack([tokens, tokens_other]), jnp.stack([tokens_other, tokens])
    ).astype(f32)
    normed_a = norm_rows(pictures, gain_a, shift_a).astype(bf16)
    mixed, heads_out, branch = attend(normed_a, full, mix_cols)
    (branch_other,) = swap(5, branch)
    resid_b = resid + (branch.astype(f32) + branch_other.astype(f32)).reshape(group, width)
    group_b = norm_rows(resid_b, gain_b, shift_b).astype(bf16)

    logits = jnp.dot(group_b, router_full, preferred_element_type=f32)
    onehot = expert_ids[:, :, None] == jnp.arange(experts, dtype=jnp.int32)[None, None, :]
    chosen = jnp.sum(jnp.where(onehot, logits[:, None, :], 0.0), axis=-1)
    pick = jax.nn.softmax(chosen, axis=-1)
    keep_float = keep_mask.astype(f32)
    gates = pick * keep_float
    dest = jnp.where(keep_mask > 0, expert_ids * slots + slot_ids, experts * slots)
    places = jnp.arange(experts * slots, dtype=jnp.int32)[None, :]
    spread = [(dest[:, j : j + 1] == places).astype(bf16) for j in range(2)]
    spread_both = spread[0] + spread[1]

    def my_columns(values):
        return lax.dynamic_slice_in_dim(values, half * half_width, half_width, 1)

    rows_sent = lax.dot_general(
        spread_both, my_columns(group_b), contract_rows, preferred_element_type=f32
    ).astype(bf16)
    grad_cols = my_columns(grad_group)
    grads_sent = sum(
        lax.dot_general(
            spread[j],
            (gates[:, j : j + 1] * grad_cols).astype(bf16),
            contract_rows,
            preferred_element_type=f32,
        )
        for j in range(2)
    ).astype(bf16)
    arrived, grad_result = dispatch(
        experts,
        rows_sent.reshape(experts, slots, half_width),
        grads_sent.reshape(experts, slots, half_width),
    )
    arrived = arrived.reshape(-1, width)
    grad_result = grad_result.reshape(-1, width)

    expand_here = w_expand[0]
    shrink_here = w_shrink[0]
    inner = jnp.dot(arrived, expand_here, preferred_element_type=f32)
    gelu_value, gelu_pull = jax.vjp(jax.nn.gelu, inner)
    active = gelu_value.astype(bf16)
    result = jnp.dot(active, shrink_here, preferred_element_type=f32).astype(bf16)
    grad_active = lax.dot_general(
        grad_result, shrink_here, contract_cols, preferred_element_type=f32
    )
    grad_inner = gelu_pull(grad_active)[0].astype(bf16)
    grad_arrived = lax.dot_general(
        grad_inner, expand_here, contract_cols, preferred_element_type=f32
    ).astype(bf16)
    back, grad_back = combine(
        experts,
        result.reshape(experts, slots, width),
        grad_arrived.reshape(experts, slots, width),
    )
    grad_shrink = lax.dot_general(active, grad_result, contract_rows, preferred_element_type=f32)
    grad_expand = lax.dot_general(arrived, grad_inner, contract_rows, preferred_element_type=f32)

    back = back.reshape(-1, half_width)
    grad_back = grad_back.reshape(-1, half_width)
    route_out = [jnp.dot(spread[j], back, preferred_element_type=f32) for j in range(2)]
    branch_cols = (gates[:, 0:1] * route_out[0] + gates[:, 1:2] * route_out[1]).astype(bf16)
    gate_part = jnp.stack([jnp.sum(grad_cols * route_out[j], axis=-1) for j in range(2)], axis=0)
    grad_cols_b = jnp.dot(spread_both, grad_back, preferred_element_type=f32).astype(bf16)
    trade = [(0, 1), (1, 0)]
    branch_theirs = lax.ppermute(branch_cols, "tensor", trade)
    grad_theirs = lax.ppermute(grad_cols_b, "tensor", trade)
    gate_theirs = lax.ppermute(gate_part, "tensor", trade)
    grad_gate = (gate_part + gate_theirs).T
    branch_b = in_order(half, branch_cols, branch_theirs, 1).astype(f32)
    grad_routes = in_order(half, grad_cols_b, grad_theirs, 1).astype(f32)
    block_out = lax.dynamic_slice_in_dim(resid_b + branch_b, half * rows, rows, 0).astype(bf16)

    grad_pick = keep_float * grad_gate
    grad_chosen = pick * (grad_pick - jnp.sum(pick * grad_pick, axis=-1, keepdims=True))
    grad_logits = jnp.sum(jnp.where(onehot, grad_chosen[:, :, None], 0.0), axis=1)
    grad_router = lax.dot_general(
        group_b.astype(f32), grad_logits, contract_rows, precision=highest
    )
    grad_normed_b = grad_routes + lax.dot_general(
        grad_logits, router_full.astype(f32), contract_cols, precision=highest
    )
    norm_value_b, norm_pull_b = jax.vjp(norm_rows, resid_b, gain_b, shift_b)
    grad_resid_b, grad_gain_b, grad_shift_b = norm_pull_b(grad_normed_b)
    grad_resid_b = grad_resid_b + grad_group

    grad_branch = grad_resid_b.astype(bf16).reshape(pictures.shape)
    grad_weights, grad_part = attend_back(
        normed_a, mixed, heads_out, grad_branch, full, mix_cols
    )
    norm_value_a, norm_pull_a = jax.vjp(norm_rows, pictures, gain_a, shift_a)
    grad_gain_a, grad_shift_a = norm_pull_a(grad_part)[1:]
    grads = jnp.concatenate(
        [
            grad_weights,
            (0.5 * grad_router).astype(bf16),
            jnp.stack(
                [grad_gain_a, grad_shift_a, 0.5 * grad_gain_b, 0.5 * grad_shift_b], axis=1
            ).astype(bf16),
            jnp.zeros((width, small - experts - 4), bf16),
        ],
        axis=1,
    ).reshape(experts, depth, -1)
    part_theirs = jnp.where(half == 0, grad_part[1], grad_part[0]).astype(bf16)
    summed, summed_small, part_got = reduce(experts, small, grads, part_theirs)
    summed_small = lax.dynamic_slice_in_dim(summed_small, half * (depth // 2), depth // 2, 0)
    grad_normed_a = jnp.where(half == 0, grad_part[0], grad_part[1]) + part_got.astype(f32)
    own = tokens.astype(f32)
    own_value, own_pull = jax.vjp(lambda values: norm_rows(values, gain_a, shift_a), own)
    grad_tokens = own_pull(grad_normed_a)[0] + lax.dynamic_slice_in_dim(
        grad_resid_b, half * rows, rows, 0
    )
    return (
        block_out,
        grad_tokens,
        summed[:, :qkv_cols].reshape(depth, 3, -1),
        summed[:, qkv_cols : qkv_cols + mix_cols],
        summed_small[:, :experts],
        summed_small[:, experts],
        summed_small[:, experts + 1],
        summed_small[:, experts + 2],
        summed_small[:, experts + 3],
        grad_expand[None],
        grad_shrink[None],
    )


def solution(mesh):
    placed = (
        P(("dp", "tensor"), None),
        P("dp", None, "tensor"),
        P("dp", "tensor"),
        P("dp", None),
        P("dp"),
        P("dp"),
        P("dp"),
        P("dp"),
        P("dp", None, "tensor"),
        P("dp", "tensor", None),
        P("dp", None),
        P("dp", None),
        P("dp", None),
        P(("dp", "tensor"), None),
    )
    return jax.shard_map(
        body,
        mesh=mesh,
        in_specs=placed,
        out_specs=(
            P(("dp", "tensor"), None),
            P(("dp", "tensor"), None),
            P("dp", None, "tensor"),
            P("dp", "tensor"),
            P(("dp", "tensor"), None),
            P(("dp", "tensor")),
            P(("dp", "tensor")),
            P(("dp", "tensor")),
            P(("dp", "tensor")),
            P("dp", None, "tensor"),
            P("dp", "tensor", None),
        ),
        check_vma=False,
    )
```

```python
import functools

import jax
import jax.numpy as jnp
from jax import lax
from jax.experimental import pallas as pl
from jax.experimental.pallas import tpu as pltpu
from jax.sharding import PartitionSpec as P

DH = 64
MESH = pl.DeviceIdType.MESH
VMEM = pl.BlockSpec(memory_space=pltpu.VMEM)
LIMIT = 48 * 1024 * 1024


def greet(peers):
    barrier = pltpu.get_barrier_semaphore()
    for peer in peers:
        pl.semaphore_signal(barrier, inc=1, device_id=peer, device_id_type=MESH)
    pl.semaphore_wait(barrier, len(peers))


def remote(src, dst, send, recv, peer):
    return pltpu.make_async_remote_copy(
        src_ref=src,
        dst_ref=dst,
        send_sem=send,
        recv_sem=recv,
        device_id=peer,
        device_id_type=MESH,
    )


def flip(me, mask):
    place = me
    bit = 1
    while bit <= mask:
        if mask & bit:
            place = place + bit - 2 * bit * lax.rem(me // bit, 2)
        bit *= 2
    return place


def low_bit(mask, n):
    return (mask & -mask) if mask else n


def bits_below(limit):
    bits = []
    bit = 1
    while bit < limit:
        bits.append(bit)
        bit *= 2
    return bits


def call(kernel, ident, outs, scratch, *operands):
    return pl.pallas_call(
        kernel,
        out_shape=outs,
        in_specs=[VMEM] * len(operands),
        out_specs=[VMEM] * len(outs),
        scratch_shapes=scratch,
        compiler_params=pltpu.CompilerParams(
            collective_id=ident, has_side_effects=True, vmem_limit_bytes=LIMIT
        ),
    )(*operands)


def shape_of(array):
    return jax.ShapeDtypeStruct(array.shape, array.dtype)


def swap_kernel(count, *refs):
    ins, outs = refs[:count], refs[count : 2 * count]
    send, recv = refs[2 * count :]
    other = {"tensor": 1 - lax.axis_index("tensor")}
    greet([other])
    copies = [remote(ins[i], outs[i], send.at[i], recv.at[i], other) for i in range(count)]
    for copy in copies:
        copy.start()
    for copy in copies:
        copy.wait()


def swap(ident, *arrays):
    count = len(arrays)
    return call(
        functools.partial(swap_kernel, count),
        ident,
        [shape_of(array) for array in arrays],
        [pltpu.SemaphoreType.DMA((count,)), pltpu.SemaphoreType.DMA((count,))],
        *arrays,
    )


def gather_kernel(n, shard, rows_a, rows_b, full, other_a, other_b, send, recv, pair_send, pair_recv, own):
    me = lax.axis_index("dp")
    other = {"tensor": 1 - lax.axis_index("tensor")}
    bits = bits_below(n)
    greet([{"dp": flip(me, bit)} for bit in bits] + [other])
    pair = [
        remote(rows_a, other_a, pair_send.at[0], pair_recv.at[0], other),
        remote(rows_b, other_b, pair_send.at[1], pair_recv.at[1], other),
    ]

    def hop(mask, bit):
        owner = flip(me, mask)
        src = shard if mask == 0 else full.at[owner]
        index = mask | bit
        return remote(
            src, full.at[owner], send.at[index], recv.at[index], {"dp": flip(me, bit)}
        )

    keep = pltpu.make_async_copy(shard, full.at[me], own)
    order = sorted(range(n), key=lambda mask: (-low_bit(mask, n), mask))
    sent = []
    for mask in order:
        if mask:
            bit = low_bit(mask, n)
            hop(mask ^ bit, bit).wait_recv()
        for bit in reversed(bits_below(low_bit(mask, n))):
            copy = hop(mask, bit)
            copy.start()
            sent.append(copy)
        if mask == 0:
            for copy in pair:
                copy.start()
            keep.start()
    keep.wait()
    for copy in sent:
        copy.wait_send()
    for copy in pair:
        copy.wait()


def gather(n, shard, rows_a, rows_b):
    return call(
        functools.partial(gather_kernel, n),
        1,
        [
            jax.ShapeDtypeStruct((n,) + shard.shape, shard.dtype),
            shape_of(rows_a),
            shape_of(rows_b),
        ],
        [
            pltpu.SemaphoreType.DMA((n,)),
            pltpu.SemaphoreType.DMA((n,)),
            pltpu.SemaphoreType.DMA((2,)),
            pltpu.SemaphoreType.DMA((2,)),
            pltpu.SemaphoreType.DMA,
        ],
        shard,
        rows_a,
        rows_b,
    )


def everyone(n, me):
    return [{"dp": lax.rem(me + k, n)} for k in range(1, n)] + [
        {"tensor": 1 - lax.axis_index("tensor")}
    ]


def dispatch_kernel(n, in_a, in_b, out_a, out_b, send, recv, pair_send, pair_recv, own):
    me = lax.axis_index("dp")
    half = lax.axis_index("tensor")
    other = {"tensor": 1 - half}
    width = in_a.shape[2]
    columns = pl.ds(pl.multiple_of(half * width, 128), width)
    ins, outs = (in_a, in_b), (out_a, out_b)
    greet(everyone(n, me))

    def direct(i, k):
        peer = lax.rem(me + k, n)
        return remote(
            ins[i].at[peer],
            outs[i].at[me, :, columns],
            send.at[i, k],
            recv.at[i, k],
            {"dp": peer},
        )

    def onward(i, k):
        part = outs[i].at[lax.rem(me - k + n, n), :, columns]
        return remote(part, part, pair_send.at[i, k], pair_recv.at[i, k], other)

    keep = [
        pltpu.make_async_copy(ins[i].at[me], outs[i].at[me, :, columns], own.at[i])
        for i in range(2)
    ]
    for i in range(2):
        keep[i].start()
        for k in range(1, n):
            direct(i, k).start()
    for i in range(2):
        keep[i].wait()
        onward(i, 0).start()
        for k in range(1, n):
            direct(i, k).wait_recv()
            onward(i, k).start()
    for i in range(2):
        for k in range(1, n):
            direct(i, k).wait_send()
        for k in range(n):
            onward(i, k).wait()


def dispatch(n, rows_a, rows_b):
    full = jax.ShapeDtypeStruct(rows_a.shape[:2] + (2 * rows_a.shape[2],), rows_a.dtype)
    return call(
        functools.partial(dispatch_kernel, n),
        2,
        [full, full],
        [pltpu.SemaphoreType.DMA((2, n)) for _ in range(4)] + [pltpu.SemaphoreType.DMA((2,))],
        rows_a,
        rows_b,
    )


def combine_kernel(
    n, in_a, in_b, out_a, out_b, got_a, got_b, sum_a, sum_b, send, recv, pair_send, pair_recv, own
):
    me = lax.axis_index("dp")
    half = lax.axis_index("tensor")
    other = {"tensor": 1 - half}
    width = out_a.shape[2]
    theirs = pl.ds(pl.multiple_of((1 - half) * width, 128), width)
    mine = pl.ds(pl.multiple_of(half * width, 128), width)
    ins, outs, gots, sums = (in_a, in_b), (out_a, out_b), (got_a, got_b), (sum_a, sum_b)
    greet(everyone(n, me))

    def across(i, k):
        block = lax.rem(me + k, n)
        return remote(
            ins[i].at[block, :, theirs],
            gots[i].at[block],
            pair_send.at[i, k],
            pair_recv.at[i, k],
            other,
        )

    def home(i, k):
        block = lax.rem(me + k, n)
        return remote(
            sums[i].at[block], outs[i].at[me], send.at[i, k], recv.at[i, k], {"dp": block}
        )

    order = list(range(1, n)) + [0]
    for i in range(2):
        for k in order:
            across(i, k).start()
    for i in range(2):
        for k in order:
            across(i, k).wait_recv()
            block = lax.rem(me + k, n)
            kept = ins[i][block, :, mine].astype(jnp.float32)
            total = (kept + gots[i][block].astype(jnp.float32)).astype(jnp.bfloat16)
            if k:
                sums[i][block] = total
                home(i, k).start()
            else:
                outs[i][block] = total
    for i in range(2):
        for k in range(n):
            across(i, k).wait_send()
        for k in range(1, n):
            home(i, k).wait()


def combine(n, parts_a, parts_b):
    size = parts_a.shape[:2] + (parts_a.shape[2] // 2,)
    out = jax.ShapeDtypeStruct(size, parts_a.dtype)
    return call(
        functools.partial(combine_kernel, n),
        3,
        [out, out],
        [pltpu.VMEM(size, parts_a.dtype) for _ in range(4)]
        + [pltpu.SemaphoreType.DMA((2, n)) for _ in range(4)]
        + [pltpu.SemaphoreType.DMA((2,))],
        parts_a,
        parts_b,
    )


def reduce_kernel(
    n, small, grads, rows, out, out_small, out_rows, got, stage, mine, theirs, send, recv, pair_send, pair_recv
):
    me = lax.axis_index("dp")
    other = {"tensor": 1 - lax.axis_index("tensor")}
    greet([{"dp": flip(me, bit)} for bit in bits_below(n)] + [other])
    pair_rows = remote(rows, out_rows, pair_send.at[0], pair_recv.at[0], other)
    pair_rows.start()

    def hop(mask):
        bit = low_bit(mask, n)
        src = grads.at[flip(me, mask)] if bit == 1 else stage.at[mask]
        return remote(src, got.at[mask], send.at[mask], recv.at[mask], {"dp": flip(me, bit)})

    def total(mask):
        value = grads[flip(me, mask)].astype(jnp.float32)
        for bit in bits_below(low_bit(mask, n)):
            hop(mask | bit).wait_recv()
            value = value + got[mask | bit].astype(jnp.float32)
        return value

    order = sorted(
        range(1, n), key=lambda mask: (low_bit(mask, n), low_bit(mask ^ low_bit(mask, n), n))
    )
    for mask in order:
        if low_bit(mask, n) > 1:
            stage[mask] = total(mask).astype(stage.dtype)
        hop(mask).start()
    value = total(0)
    out[...] = value
    mine[...] = value[:, value.shape[1] - small :]
    pair_small = remote(mine, theirs, pair_send.at[1], pair_recv.at[1], other)
    pair_small.start()
    for mask in order:
        hop(mask).wait_send()
    pair_small.wait()
    out_small[...] = mine[...] + theirs[...]
    pair_rows.wait()


def reduce(n, small, grads, rows):
    depth, columns = grads.shape[1:]
    return call(
        functools.partial(reduce_kernel, n, small),
        4,
        [
            jax.ShapeDtypeStruct((depth, columns), jnp.float32),
            jax.ShapeDtypeStruct((depth, small), jnp.float32),
            shape_of(rows),
        ],
        [
            pltpu.VMEM(grads.shape, grads.dtype),
            pltpu.VMEM(grads.shape, grads.dtype),
            pltpu.VMEM((depth, small), jnp.float32),
            pltpu.VMEM((depth, small), jnp.float32),
            pltpu.SemaphoreType.DMA((n,)),
            pltpu.SemaphoreType.DMA((n,)),
            pltpu.SemaphoreType.DMA((2,)),
            pltpu.SemaphoreType.DMA((2,)),
        ],
        grads,
        rows,
    )


def in_order(half, mine, theirs, axis):
    first = jnp.where(half == 0, mine, theirs)
    second = jnp.where(half == 0, theirs, mine)
    return jnp.concatenate([first, second], axis=axis)


def norm_rows(values, gain, shift):
    centre = values - jnp.mean(values, axis=-1, keepdims=True)
    spread = jnp.mean(centre * centre, axis=-1, keepdims=True)
    return centre * lax.rsqrt(spread + 1e-06) * gain + shift


def softmax_rows(query, key_rows):
    scores = lax.dot_general(
        query, key_rows, (((1,), (1,)), ((), ())), preferred_element_type=jnp.float32
    ) * DH ** (-0.5)
    powers = jnp.exp(scores - jnp.max(scores, axis=-1, keepdims=True))
    return powers / jnp.sum(powers, axis=-1, keepdims=True)


def attend_kernel(wide, normed, full, mixed, heads_out, branch):
    for image in range(normed.shape[0]):
        mixed[image] = jnp.dot(
            normed[image], full[:, : 3 * wide], preferred_element_type=jnp.float32
        ).astype(jnp.bfloat16)
        outs = []
        for at in range(0, wide, DH):
            query, key_rows, value_rows = (
                mixed[image, :, part * wide + at : part * wide + at + DH] for part in range(3)
            )
            weights = softmax_rows(query, key_rows).astype(jnp.bfloat16)
            outs.append(jnp.dot(weights, value_rows, preferred_element_type=jnp.float32))
        heads_out[image] = jnp.concatenate(outs, axis=1).astype(jnp.bfloat16)
        length = normed.shape[1]
        branch[image * length : (image + 1) * length, :] = lax.dot_general(
            heads_out[image],
            full[:, 3 * wide : 4 * wide],
            (((1,), (1,)), ((), ())),
            preferred_element_type=jnp.float32,
        ).astype(jnp.bfloat16)


def attend_back_kernel(
    wide, normed, mixed, heads_out, grad_branch, full, grads, grad_part, grad_mixed, grad_heads
):
    rows = (((0,), (0,)), ((), ()))
    cols = (((1,), (1,)), ((), ()))
    f32 = jnp.float32
    scale = DH ** (-0.5)
    for image in range(normed.shape[0]):
        grad_heads[image] = jnp.dot(
            grad_branch[image], full[:, 3 * wide : 4 * wide], preferred_element_type=f32
        ).astype(jnp.bfloat16)
        parts = ([], [], [])
        for at in range(0, wide, DH):
            query, key_rows, value_rows = (
                mixed[image, :, part * wide + at : part * wide + at + DH] for part in range(3)
            )
            probs = softmax_rows(query, key_rows)
            grad_out = grad_heads[image, :, at : at + DH]
            grad_probs = lax.dot_general(grad_out, value_rows, cols, preferred_element_type=f32)
            parts[2].append(
                lax.dot_general(
                    probs.astype(jnp.bfloat16), grad_out, rows, preferred_element_type=f32
                )
            )
            grad_scores = (
                probs * (grad_probs - jnp.sum(probs * grad_probs, axis=-1, keepdims=True))
            ).astype(jnp.bfloat16)
            parts[0].append(jnp.dot(grad_scores, key_rows, preferred_element_type=f32) * scale)
            parts[1].append(
                lax.dot_general(grad_scores, query, rows, preferred_element_type=f32) * scale
            )
        grad_mixed[image] = jnp.concatenate(parts[0] + parts[1] + parts[2], axis=1).astype(
            jnp.bfloat16
        )
        grad_part[image] = lax.dot_general(
            grad_mixed[image], full[:, : 3 * wide], cols, preferred_element_type=f32
        )
    images = range(normed.shape[0])
    grads[:, : 3 * wide] = sum(
        lax.dot_general(normed[i], grad_mixed[i], rows, preferred_element_type=f32) for i in images
    ).astype(jnp.bfloat16)
    grads[:, 4 * wide :] = jnp.zeros((grads.shape[0], grads.shape[1] - 4 * wide), grads.dtype)
    grads[:, 3 * wide : 4 * wide] = sum(
        lax.dot_general(grad_branch[i], heads_out[i], rows, preferred_element_type=f32)
        for i in images
    ).astype(jnp.bfloat16)


def local_call(kernel, outs, scratch, *operands):
    return pl.pallas_call(
        kernel,
        out_shape=outs,
        in_specs=[VMEM] * len(operands),
        out_specs=[VMEM] * len(outs),
        scratch_shapes=scratch,
        compiler_params=pltpu.CompilerParams(vmem_limit_bytes=LIMIT),
    )(*operands)


def attend(normed, full, wide):
    images, length, width = normed.shape
    sizes = ((images, length, 3 * wide), (images, length, wide), (images * length, width))
    return local_call(
        functools.partial(attend_kernel, wide),
        [jax.ShapeDtypeStruct(size, jnp.bfloat16) for size in sizes],
        [],
        normed,
        full,
    )


def attend_back(normed, mixed, heads_out, grad_branch, full, wide):
    images, length, width = normed.shape
    return local_call(
        functools.partial(attend_back_kernel, wide),
        [
            jax.ShapeDtypeStruct((width, full.shape[1]), jnp.bfloat16),
            jax.ShapeDtypeStruct(normed.shape, jnp.float32),
        ],
        [pltpu.VMEM(mixed.shape, mixed.dtype), pltpu.VMEM(heads_out.shape, heads_out.dtype)],
        normed,
        mixed,
        heads_out,
        grad_branch,
        full,
    )


def body(
    tokens,
    w_qkv,
    w_mix,
    w_router,
    gain_one,
    shift_one,
    gain_two,
    shift_two,
    w_expand,
    w_shrink,
    expert_ids,
    slot_ids,
    keep_mask,
    out_grad,
):
    highest = lax.Precision.HIGHEST
    contract_rows = (((0,), (0,)), ((), ()))
    contract_cols = (((1,), (1,)), ((), ()))
    bf16 = jnp.bfloat16
    f32 = jnp.float32
    rows, width = tokens.shape
    group = expert_ids.shape[0]
    experts = lax.axis_size("dp")
    half = lax.axis_index("tensor")
    slots = 2 * max(1, 2 * group * 2 // 3 // experts)
    depth = w_qkv.shape[0]
    qkv_cols = 3 * w_qkv.shape[2]
    mix_cols = w_mix.shape[1]
    half_width = width // 2
    small = -(-(experts + 4) // 128) * 128

    vectors = jnp.stack([gain_one, shift_one, gain_two, shift_two], axis=1)
    shard = jnp.concatenate(
        [
            w_qkv.reshape(depth, qkv_cols),
            w_mix,
            w_router,
            vectors,
            jnp.zeros((depth, small - experts - 4), bf16),
        ],
        axis=1,
    )
    full, tokens_other, grad_other = gather(experts, shard, tokens, out_grad)
    full = full.reshape(experts * depth, -1)
    router_full = full[:, qkv_cols + mix_cols : qkv_cols + mix_cols + experts]
    vectors = full[:, qkv_cols + mix_cols + experts : qkv_cols + mix_cols + experts + 4]
    gain_a, shift_a, gain_b, shift_b = vectors.astype(f32).T
    resid = in_order(half, tokens, tokens_other, 0).astype(f32)
    grad_group = in_order(half, out_grad, grad_other, 0).astype(f32)

    pictures = jnp.where(
        half == 0, jnp.stack([tokens, tokens_other]), jnp.stack([tokens_other, tokens])
    ).astype(f32)
    normed_a = norm_rows(pictures, gain_a, shift_a).astype(bf16)
    mixed, heads_out, branch = attend(normed_a, full, mix_cols)
    (branch_other,) = swap(5, branch)
    resid_b = resid + (branch.astype(f32) + branch_other.astype(f32))
    group_b = norm_rows(resid_b, gain_b, shift_b).astype(bf16)

    logits = jnp.dot(group_b, router_full, preferred_element_type=f32)
    onehot = expert_ids[:, :, None] == jnp.arange(experts, dtype=jnp.int32)[None, None, :]
    chosen = jnp.sum(jnp.where(onehot, logits[:, None, :], 0.0), axis=-1)
    pick = jax.nn.softmax(chosen, axis=-1)
    keep_float = keep_mask.astype(f32)
    gates = pick * keep_float
    dest = jnp.where(keep_mask > 0, expert_ids * slots + slot_ids, experts * slots)
    places = jnp.arange(experts * slots, dtype=jnp.int32)[None, :]
    spread = [(dest[:, j : j + 1] == places).astype(bf16) for j in range(2)]
    spread_both = spread[0] + spread[1]

    def my_columns(values):
        return lax.dynamic_slice_in_dim(values, half * half_width, half_width, 1)

    rows_sent = lax.dot_general(
        spread_both, my_columns(group_b), contract_rows, preferred_element_type=f32
    ).astype(bf16)
    grad_cols = my_columns(grad_group)
    grads_sent = sum(
        lax.dot_general(
            spread[j],
            (gates[:, j : j + 1] * grad_cols).astype(bf16),
            contract_rows,
            preferred_element_type=f32,
        )
        for j in range(2)
    ).astype(bf16)
    arrived, grad_result = dispatch(
        experts,
        rows_sent.reshape(experts, slots, half_width),
        grads_sent.reshape(experts, slots, half_width),
    )
    arrived = arrived.reshape(-1, width)
    grad_result = grad_result.reshape(-1, width)

    expand_here = w_expand[0]
    shrink_here = w_shrink[0]
    inner = jnp.dot(arrived, expand_here, preferred_element_type=f32)
    gelu_value, gelu_pull = jax.vjp(jax.nn.gelu, inner)
    active = gelu_value.astype(bf16)
    result = jnp.dot(active, shrink_here, preferred_element_type=f32).astype(bf16)
    grad_active = lax.dot_general(
        grad_result, shrink_here, contract_cols, preferred_element_type=f32
    )
    grad_inner = gelu_pull(grad_active)[0].astype(bf16)
    grad_arrived = lax.dot_general(
        grad_inner, expand_here, contract_cols, preferred_element_type=f32
    ).astype(bf16)
    back, grad_back = combine(
        experts,
        result.reshape(experts, slots, width),
        grad_arrived.reshape(experts, slots, width),
    )
    grad_shrink = lax.dot_general(active, grad_result, contract_rows, preferred_element_type=f32)
    grad_expand = lax.dot_general(arrived, grad_inner, contract_rows, preferred_element_type=f32)

    back = back.reshape(-1, half_width)
    grad_back = grad_back.reshape(-1, half_width)
    route_out = [jnp.dot(spread[j], back, preferred_element_type=f32) for j in range(2)]
    branch_cols = (gates[:, 0:1] * route_out[0] + gates[:, 1:2] * route_out[1]).astype(bf16)
    gate_part = jnp.stack([jnp.sum(grad_cols * route_out[j], axis=-1) for j in range(2)], axis=0)
    grad_cols_b = jnp.dot(spread_both, grad_back, preferred_element_type=f32).astype(bf16)
    trade = [(0, 1), (1, 0)]
    branch_theirs = lax.ppermute(branch_cols, "tensor", trade)
    grad_theirs = lax.ppermute(grad_cols_b, "tensor", trade)
    gate_theirs = lax.ppermute(gate_part, "tensor", trade)
    grad_gate = (gate_part + gate_theirs).T
    branch_b = in_order(half, branch_cols, branch_theirs, 1).astype(f32)
    grad_routes = in_order(half, grad_cols_b, grad_theirs, 1).astype(f32)
    block_out = lax.dynamic_slice_in_dim(resid_b + branch_b, half * rows, rows, 0).astype(bf16)

    grad_pick = keep_float * grad_gate
    grad_chosen = pick * (grad_pick - jnp.sum(pick * grad_pick, axis=-1, keepdims=True))
    grad_logits = jnp.sum(jnp.where(onehot, grad_chosen[:, :, None], 0.0), axis=1)
    grad_router = lax.dot_general(
        group_b.astype(f32), grad_logits, contract_rows, precision=highest
    )
    grad_normed_b = grad_routes + lax.dot_general(
        grad_logits, router_full.astype(f32), contract_cols, precision=highest
    )
    norm_value_b, norm_pull_b = jax.vjp(norm_rows, resid_b, gain_b, shift_b)
    grad_resid_b, grad_gain_b, grad_shift_b = norm_pull_b(grad_normed_b)
    grad_resid_b = grad_resid_b + grad_group

    grad_branch = grad_resid_b.astype(bf16).reshape(pictures.shape)
    grad_weights, grad_part = attend_back(
        normed_a, mixed, heads_out, grad_branch, full, mix_cols
    )
    norm_value_a, norm_pull_a = jax.vjp(norm_rows, pictures, gain_a, shift_a)
    grad_gain_a, grad_shift_a = norm_pull_a(grad_part)[1:]
    small_grads = jnp.concatenate(
        [
            (0.5 * grad_router).astype(bf16),
            jnp.stack(
                [grad_gain_a, grad_shift_a, 0.5 * grad_gain_b, 0.5 * grad_shift_b], axis=1
            ).astype(bf16),
            jnp.zeros((width, small - experts - 4), bf16),
        ],
        axis=1,
    )
    grads = lax.dynamic_update_slice(grad_weights, small_grads, (0, qkv_cols + mix_cols))
    grads = grads.reshape(experts, depth, -1)
    part_theirs = jnp.where(half == 0, grad_part[1], grad_part[0]).astype(bf16)
    summed, summed_small, part_got = reduce(experts, small, grads, part_theirs)
    summed_small = lax.dynamic_slice_in_dim(summed_small, half * (depth // 2), depth // 2, 0)
    grad_normed_a = jnp.where(half == 0, grad_part[0], grad_part[1]) + part_got.astype(f32)
    own = tokens.astype(f32)
    own_value, own_pull = jax.vjp(lambda values: norm_rows(values, gain_a, shift_a), own)
    grad_tokens = own_pull(grad_normed_a)[0] + lax.dynamic_slice_in_dim(
        grad_resid_b, half * rows, rows, 0
    )
    return (
        block_out,
        grad_tokens,
        summed[:, :qkv_cols].reshape(depth, 3, -1),
        summed[:, qkv_cols : qkv_cols + mix_cols],
        summed_small[:, :experts],
        summed_small[:, experts],
        summed_small[:, experts + 1],
        summed_small[:, experts + 2],
        summed_small[:, experts + 3],
        grad_expand[None],
        grad_shrink[None],
    )


def solution(mesh):
    placed = (
        P(("dp", "tensor"), None),
        P("dp", None, "tensor"),
        P("dp", "tensor"),
        P("dp", None),
        P("dp"),
        P("dp"),
        P("dp"),
        P("dp"),
        P("dp", None, "tensor"),
        P("dp", "tensor", None),
        P("dp", None),
        P("dp", None),
        P("dp", None),
        P(("dp", "tensor"), None),
    )
    return jax.shard_map(
        body,
        mesh=mesh,
        in_specs=placed,
        out_specs=(
            P(("dp", "tensor"), None),
            P(("dp", "tensor"), None),
            P("dp", None, "tensor"),
            P("dp", "tensor"),
            P(("dp", "tensor"), None),
            P(("dp", "tensor")),
            P(("dp", "tensor")),
            P(("dp", "tensor")),
            P(("dp", "tensor")),
            P("dp", None, "tensor"),
            P("dp", "tensor", None),
        ),
        check_vma=False,
    )
```
